512 devices in a mesh: beam: 32 (over x_hi, z), band: 16 (over x_lo, y, core).
Axes of the slice: x: 4 (x_hi: 2, x_lo: 2; x = x_hi * 2 + x_lo), y: 4, z: 16, core: 2. Of those that a mesh axis runs over, the one named last changes fastest.
Arguments:
- intensity: bfloat16 [1280, 32, 4096], P('beam', None, 'band'), may hold values from -6 to 6
- chan_shift: int32 [32, 4096], P(None, 'band'), may hold values from 0 to 1
- sub_shift: int32 [1024, 256], replicated, may hold values from 0 to 5
- widths: int32 [16], replicated, may hold values from 1 to 128, as said below
Outputs:
- dm_series: bfloat16 [1024, 32, 512], P('band', 'beam')
- snr_peak: float32 [32, 16, 4], P('beam')
The draws below stay inside these ranges and needn't reach their ends.
Inputs may be any that keep to these rules, and one draw needn't show every extreme that they name: `widths`: one boxcar has 128 samples and one has 1.
All inputs are finite; a program needn't handle non-finite values.
Results may differ from the reference program's by a relative error of at most 0.005.
Values may be sent and summed in bfloat16 or wider, within the bound.
A program may use at most 64 MiB of HBM per device.

```python
import math
import jax
import jax.numpy as jnp
from jax import lax

CHANNELS = 4096
CHSUB = 16
DMG = 32
DMF = 32
TILE = 128
OUT_TILES = 4
CH_SHIFTS = 2
SUB_SHIFTS = 6
NBOX = 16
MAXW = 128
BEAMS = 32
SUBBANDS = 256
DMS = 1024
TIME = 512
MID_TILES = 9
TIME_IN = 1280


def draw_widths(key, part):
    key = jax.random.fold_in(key, 7)
    first_key, second_key = jax.random.split(key)
    values = jax.random.randint(first_key, (NBOX,), 1, MAXW + 1)
    places = jax.random.permutation(second_key, NBOX)
    values = values.at[places[0]].set(MAXW)
    values = values.at[places[1]].set(1)
    return values.astype(jnp.int32)


def place_ends(entries, stream_key, smallest, high):
    dims = entries.shape
    spot = [jax.random.randint(jax.random.fold_in(stream_key, axis), (), 0, dims[axis]) for axis in range(len(dims))]
    entries = entries.at[tuple(spot)].set(smallest)
    longest = dims.index(max(dims))
    spot[longest] = (spot[longest] + 1) % dims[longest]
    return entries.at[tuple(spot)].set(high)


def block_levels(key, shape, pieces, low, largest):
    loudness = 1.0
    for dim, shards_of in pieces:
        draws = jax.random.uniform(jax.random.fold_in(jax.random.fold_in(key, 6), dim), (shards_of,), jnp.float32, low / len(pieces), largest / len(pieces))
        loudness = loudness * jnp.repeat(jnp.exp(draws), shape[dim] // shards_of).reshape((-1,) + (1,) * (len(shape) - 1 - dim))
    return loudness


def gaussian(rng, extent, width, reach, cuts=(), held_as=jnp.bfloat16):
    result = width * jax.random.normal(rng, extent, jnp.float32)
    if cuts:
        result = result * block_levels(rng, extent, cuts, -0.22, 0.18)
    return jnp.clip(result, -reach, reach).astype(held_as)


def setup_inputs(seed: int = 0) -> dict:
    keys = jax.random.split(jax.random.key(seed), 5)
    intensity = gaussian(keys[0], (TIME_IN, BEAMS, CHANNELS), 1.0, 6.0, ((0, 32), (2, 16)))
    chan_shift = place_ends(jax.random.randint(keys[1], (DMG, CHANNELS), 0, CH_SHIFTS), jax.random.fold_in(keys[1], 1), 0, CH_SHIFTS - 1).astype(jnp.int32)
    sub_shift = place_ends(jax.random.randint(keys[2], (DMS, SUBBANDS), 0, SUB_SHIFTS), jax.random.fold_in(keys[2], 1), 0, SUB_SHIFTS - 1).astype(jnp.int32)
    widths = draw_widths(jax.random.fold_in(keys[4], 71), 0)
    return {"intensity": intensity, "chan_shift": chan_shift, "sub_shift": sub_shift, "widths": widths}


EPSILON = 1e-05

def subband_series(beam_data, chan_shift):
    spread = beam_data.astype(jnp.float32).reshape(SUBBANDS, CHSUB, TIME_IN)
    shift_table = chan_shift.reshape(DMG, SUBBANDS, CHSUB)
    summed = jnp.zeros((DMG, SUBBANDS, MID_TILES * TILE), jnp.float32)
    for offset in range(CH_SHIFTS):
        selector = (shift_table == offset).astype(jnp.float32)
        window = spread[:, :, offset * TILE:offset * TILE + MID_TILES * TILE]
        summed = summed + jnp.einsum('gsq,sqt->gst', selector, window)
    return summed.astype(jnp.bfloat16)

def trial_series(subseries, sub_shift):
    spread = subseries.astype(jnp.float32)
    shift_table = sub_shift.reshape(DMG, DMF, SUBBANDS)
    summed = jnp.zeros((DMG, DMF, TIME), jnp.float32)
    for offset in range(SUB_SHIFTS):
        selector = (shift_table == offset).astype(jnp.float32)
        window = spread[:, :, offset * TILE:offset * TILE + TIME]
        summed = summed + jnp.einsum('gfs,gst->gft', selector, window)
    scaled = summed.reshape(DMS, TIME) * (1.0 / math.sqrt(CHANNELS))
    return scaled.astype(jnp.bfloat16)

def peak_ratio(dm_rows, widths):
    values = dm_rows.astype(jnp.float32)
    centre = lax.optimization_barrier(jnp.mean(values, axis=1, keepdims=True))
    spread = lax.optimization_barrier(jnp.mean((values - centre) ** 2, axis=1, keepdims=True))
    rounded = lax.optimization_barrier(((values - centre) / jnp.sqrt(spread + EPSILON)).astype(jnp.bfloat16))
    normed = rounded.astype(jnp.float32)
    prefix = jnp.concatenate([jnp.zeros((DMS, 1), jnp.float32), jnp.cumsum(normed, axis=1)], axis=1)
    sample_index = jnp.arange(TIME, dtype=jnp.int32)

    def one_width(box_width):
        lower_edge = jnp.maximum(sample_index + 1 - box_width, 0).astype(jnp.int32)
        box_sum = prefix[:, 1:] - jnp.take(prefix, lower_edge, axis=1)
        ratio = box_sum / jnp.sqrt(box_width.astype(jnp.float32))
        return lax.optimization_barrier(jnp.max(ratio.reshape(DMS, OUT_TILES, TILE), axis=(0, 2)))
    return lax.map(one_width, widths)

def reference(intensity, chan_shift, sub_shift, widths):

    def one_beam(beam_number):
        column = lax.dynamic_index_in_dim(intensity, beam_number, 1, keepdims=False)
        beam_data = jnp.transpose(column, (1, 0))
        subseries = subband_series(beam_data, chan_shift)
        dm_rows = trial_series(subseries, sub_shift)
        return (dm_rows, peak_ratio(dm_rows, widths))
    dm_all, peaks = lax.map(one_beam, jnp.arange(BEAMS, dtype=jnp.int32))
    return (jnp.transpose(dm_all, (1, 0, 2)), peaks)
```

```python
import jax
import jax.numpy as jnp
from jax import lax
from jax.experimental import pallas as pl
from jax.experimental.pallas import tpu as pltpu
from jax.sharding import PartitionSpec as P

MESH = pl.DeviceIdType.MESH
F32 = jnp.float32
BF16 = jnp.bfloat16
LANES = 128
SAMPLES = 40
BEAMS = 32
BANDS = 16
HALVES = 2
GROUPS = 32
SUB_ROWS = 16
TILES_IN = 10
TILES_MID = 9
TILES_OUT = 4
SHIFTS = 6
OWN = 64
NBOX = 16
EPSILON = 1e-05


def dot(a, b):
    return lax.dot_general(a, b, (((1,), (0,)), ((), ())), preferred_element_type=F32)


def dot_t(a, b):
    return lax.dot_general(a, b, (((1,), (1,)), ((), ())), preferred_element_type=F32)


def kernel(
    x_ref, chan_ref, shift_ref, width_ref, dm_ref, peak_ref,
    wide, block, got, chan_sel, shift_own, shift_sel, series, held, box, root, total, peaks, peaks_in,
    load_sem, beam_send, beam_recv, band_send, band_recv, peak_send, peak_recv,
):
    me = lax.axis_index("beam")
    band = lax.axis_index("band")

    barrier = pltpu.get_barrier_semaphore()

    def greet_beam(i, _):
        pl.semaphore_signal(barrier, inc=1, device_id=(lax.rem(me + i, BEAMS), band), device_id_type=MESH)
        return 0

    def greet_band(i, _):
        pl.semaphore_signal(barrier, inc=1, device_id=(me, lax.rem(band + i, BANDS)), device_id_type=MESH)
        return 0

    lax.fori_loop(1, BEAMS, greet_beam, 0)
    lax.fori_loop(1, BANDS, greet_band, 0)

    own_shift = pltpu.make_async_copy(shift_ref.at[pl.ds(band * OWN, OWN)], shift_own, load_sem)
    own_shift.start()

    def widen(i, _):
        for h in range(HALVES):
            part = x_ref[pl.ds(i * 8, 8), :, h * LANES : (h + 1) * LANES]
            wide[h, pl.ds(pl.multiple_of(i * 8 * BEAMS, 8 * BEAMS), 8 * BEAMS), :] = part.astype(F32).reshape(8 * BEAMS, LANES)
        return 0

    lax.fori_loop(0, SAMPLES // 8, widen, 0)

    def pick(b, _):
        for h in range(HALVES):
            block[h, b] = wide.at[h][pl.ds(b, SAMPLES, stride=BEAMS), :].astype(BF16)
        return 0

    lax.fori_loop(0, BEAMS, pick, 0)

    pl.semaphore_wait(barrier, BEAMS - 1 + BANDS - 1)

    for h in range(HALVES):
        def send_beam(i, _):
            peer = lax.rem(me + i, BEAMS)
            pltpu.make_async_remote_copy(
                src_ref=block.at[h, peer], dst_ref=got.at[h, me],
                send_sem=beam_send.at[h], recv_sem=beam_recv.at[h],
                device_id=(peer, band), device_id_type=MESH,
            ).start()
            return 0

        lax.fori_loop(1, BEAMS, send_beam, 0)
        got[h, me] = block[h, me]

    row = lax.broadcasted_iota(jnp.int32, (GROUPS * 8, LANES), 0)
    lane = lax.broadcasted_iota(jnp.int32, (GROUPS * 8, LANES), 1)
    mine = lax.rem(row, 8) == lane // 16
    for h in range(HALVES):
        delays = chan_ref[:, h * LANES : (h + 1) * LANES]
        delays = jnp.broadcast_to(delays[:, None, :], (GROUPS, 8, LANES)).reshape(GROUPS * 8, LANES)
        for k in range(2):
            chan_sel[h, :, k * LANES : (k + 1) * LANES] = jnp.where(mine & (delays == k), 1.0, 0.0).astype(BF16)

    own_shift.wait()
    col = lax.broadcasted_iota(jnp.int32, (32, 256), 1)
    high = lax.rem(col // 8, 2) == 1
    for h in range(HALVES):
        first, second = shift_own[0:32, :], shift_own[32:64, :]
        if h == 0:
            second = pltpu.roll(second, 8, 1)
        else:
            first = pltpu.roll(first, 256 - 8, 1)
        for k in range(SHIFTS):
            shift_sel[h, k * OWN : k * OWN + 32, :] = jnp.where((first == k) & jnp.logical_not(high), 1.0, 0.0).astype(BF16)
            shift_sel[h, k * OWN + 32 : (k + 1) * OWN, :] = jnp.where((second == k) & high, 1.0, 0.0).astype(BF16)

    lag = (
        lax.broadcasted_iota(jnp.int32, (256, LANES), 1) + LANES
        - lax.broadcasted_iota(jnp.int32, (256, LANES), 0)
    )
    which = lax.broadcasted_iota(jnp.int32, (NBOX, LANES), 0)
    scale = jnp.ones((NBOX, LANES), F32)
    for i in range(NBOX):
        width = width_ref[i]
        box[:, i * LANES : (i + 1) * LANES] = jnp.where((lag >= 0) & (lag < width), 1.0, 0.0).astype(BF16)
        scale = jnp.where(which == i, width.astype(F32), scale)
    root[...] = jnp.sqrt(scale)

    total[...] = jnp.zeros_like(total)

    def arrived(buffer, sem):
        pltpu.make_async_copy(buffer, buffer, sem).wait()

    def subseries(h):
        arrived(got.at[h, pl.ds(0, BEAMS - 1)], beam_recv.at[h])
        data = got[h].astype(F32).reshape(BEAMS * SAMPLES, LANES).astype(BF16)
        for first, count in ((0, 4), (4, 5)):
            rows = count * LANES
            pair = jnp.concatenate(
                [data[first * LANES : first * LANES + rows], data[(first + 1) * LANES : (first + 1) * LANES + rows]], axis=1
            )
            summed = dot_t(chan_sel[h], pair).astype(BF16)
            for i in range(count):
                series[h, :, first + i] = summed[:, i * LANES : (i + 1) * LANES].reshape(BANDS, SUB_ROWS, LANES)

        def send_band(i, _):
            peer = lax.rem(band + i, BANDS)
            pltpu.make_async_remote_copy(
                src_ref=series.at[h, peer], dst_ref=held.at[h, band],
                send_sem=band_send.at[h], recv_sem=band_recv.at[h],
                device_id=(me, peer), device_id_type=MESH,
            ).start()
            return 0

        lax.fori_loop(1, BANDS, send_band, 0)
        held[h, band] = series[h, band]

    def trials(h):
        arrived(held.at[h, pl.ds(0, BANDS - 1)], band_recv.at[h])
        for tile in range(0, TILES_MID, 2):
            tiles = [t for t in (tile, tile + 1) if t < TILES_MID]
            low = max(0, tiles[0] - TILES_OUT + 1)
            top = min(SHIFTS - 1, tiles[-1])
            data = jnp.concatenate([held[h, :, t].reshape(BANDS * SUB_ROWS, LANES) for t in tiles], axis=1)
            part = dot(shift_sel[h, low * OWN : (top + 1) * OWN, :], data)
            for n, t in enumerate(tiles):
                for k in range(low, top + 1):
                    o = t - k
                    if 0 <= o < TILES_OUT:
                        total[:, o * LANES : (o + 1) * LANES] += part[
                            (k - low) * OWN : (k - low + 1) * OWN, n * LANES : (n + 1) * LANES
                        ]

    subseries(0)
    trials(0)
    subseries(1)
    trials(1)

    dm = (total[...] * (1.0 / 64.0)).astype(BF16)
    dm_ref[...] = dm
    values = dm.astype(F32)
    centre = jnp.mean(values, axis=1, keepdims=True)
    off = values - centre
    spread = jnp.mean(off * off, axis=1, keepdims=True)
    normed = (off / jnp.sqrt(spread + EPSILON)).astype(BF16)
    before = jnp.concatenate([jnp.zeros((OWN, LANES), BF16), normed[:, : 3 * LANES]], axis=1)
    pairs = jnp.concatenate(
        [
            jnp.concatenate([before[:, k * LANES : (k + 1) * LANES], normed[:, k * LANES : (k + 1) * LANES]], axis=1)
            for k in range(TILES_OUT)
        ],
        axis=0,
    )
    best = [[] for _ in range(TILES_OUT)]
    for i in range(0, NBOX, 2):
        sums = dot(pairs, box[:, i * LANES : (i + 2) * LANES])
        for k in range(TILES_OUT):
            top = jnp.max(sums[k * OWN : (k + 1) * OWN].reshape(8, 8, 2 * LANES), axis=0)
            best[k] += [top[:, :LANES], top[:, LANES:]]
    place = lax.broadcasted_iota(jnp.int32, (NBOX, LANES), 1)
    found = jnp.zeros((NBOX, LANES), F32)
    for k in range(TILES_OUT):
        rows = jnp.max(jnp.stack(best[k], axis=0), axis=1)
        found = jnp.where(place == k, jnp.max(rows, axis=1, keepdims=True), found)
    peaks[...] = found / root[...]

    def send_peak(i, _):
        peer = lax.rem(band + i, BANDS)
        pltpu.make_async_remote_copy(
            src_ref=peaks, dst_ref=peaks_in.at[band],
            send_sem=peak_send, recv_sem=peak_recv,
            device_id=(me, peer), device_id_type=MESH,
        ).start()
        return 0

    lax.fori_loop(1, BANDS, send_peak, 0)
    peaks_in[band] = peaks[...]
    for h in range(HALVES):
        arrived(block.at[h, pl.ds(0, BEAMS - 1)], beam_send.at[h])
        arrived(series.at[h, pl.ds(0, BANDS - 1)], band_send.at[h])
    arrived(peaks_in.at[pl.ds(0, BANDS - 1)], peak_recv)
    peak_ref[...] = jnp.max(peaks_in[...], axis=0)[:, :TILES_OUT]
    arrived(peaks_in.at[pl.ds(0, BANDS - 1)], peak_send)


def local(intensity, chan_shift, sub_shift, widths):
    vmem = pl.BlockSpec(memory_space=pltpu.VMEM)
    dm, peak = pl.pallas_call(
        kernel,
        out_shape=(
            jax.ShapeDtypeStruct((OWN, TILES_OUT * LANES), BF16),
            jax.ShapeDtypeStruct((NBOX, TILES_OUT), F32),
        ),
        in_specs=[vmem, vmem, pl.BlockSpec(memory_space=pl.ANY), pl.BlockSpec(memory_space=pltpu.SMEM)],
        out_specs=(vmem, vmem),
        scratch_shapes=[
            pltpu.VMEM((HALVES, SAMPLES * BEAMS, LANES), F32),
            pltpu.VMEM((HALVES, BEAMS, SAMPLES, LANES), BF16),
            pltpu.VMEM((HALVES, BEAMS, SAMPLES, LANES), BF16),
            pltpu.VMEM((HALVES, GROUPS * 8, 2 * LANES), BF16),
            pltpu.VMEM((OWN, 256), jnp.int32),
            pltpu.VMEM((HALVES, SHIFTS * OWN, 256), BF16),
            pltpu.VMEM((HALVES, BANDS, TILES_MID, SUB_ROWS, LANES), BF16),
            pltpu.VMEM((HALVES, BANDS, TILES_MID, SUB_ROWS, LANES), BF16),
            pltpu.VMEM((256, NBOX * LANES), BF16),
            pltpu.VMEM((NBOX, LANES), F32),
            pltpu.VMEM((OWN, TILES_OUT * LANES), F32),
            pltpu.VMEM((NBOX, LANES), F32),
            pltpu.VMEM((BANDS, NBOX, LANES), F32),
            pltpu.SemaphoreType.DMA,
            pltpu.SemaphoreType.DMA((HALVES,)),
            pltpu.SemaphoreType.DMA((HALVES,)),
            pltpu.SemaphoreType.DMA((HALVES,)),
            pltpu.SemaphoreType.DMA((HALVES,)),
            pltpu.SemaphoreType.DMA,
            pltpu.SemaphoreType.DMA,
        ],
        compiler_params=pltpu.CompilerParams(
            collective_id=0, has_side_effects=True, vmem_limit_bytes=48 << 20
        ),
        cost_estimate=pl.CostEstimate(flops=4_000_000_000, bytes_accessed=2_000_000, transcendentals=0),
    )(intensity, chan_shift, sub_shift, widths)
    return dm.reshape(OWN, 1, TILES_OUT * LANES), peak.reshape(1, NBOX, TILES_OUT)


def solution(mesh):
    return jax.shard_map(
        local,
        mesh=mesh,
        in_specs=(P("beam", None, "band"), P(None, "band"), P(), P()),
        out_specs=(P("band", "beam", None), P("beam", None, None)),
        check_vma=False,
    )
```

```python
import jax
import jax.numpy as jnp
from jax import lax
from jax.experimental import pallas as pl
from jax.experimental.pallas import tpu as pltpu
from jax.sharding import PartitionSpec as P

MESH = pl.DeviceIdType.MESH
F32 = jnp.float32
BF16 = jnp.bfloat16
LANES = 128
SAMPLES = 40
BEAMS = 32
RING = 16
BANDS = 16
HALVES = 2
GROUPS = 32
SUB_ROWS = 16
TILES_IN = 10
TILES_MID = 9
TILES_OUT = 4
SHIFTS = 6
OWN = 64
NBOX = 16
EPSILON = 1e-05


def dot(a, b):
    return lax.dot_general(a, b, (((1,), (0,)), ((), ())), preferred_element_type=F32)


def dot_t(a, b):
    return lax.dot_general(a, b, (((1,), (1,)), ((), ())), preferred_element_type=F32)


def kernel(
    x_hbm, chan_hbm, shift_hbm, width_hbm, dm_ref, peak_ref,
    x_ref, chan_ref, width_ref, wide, block, got, chan_sel, shift_own, shift_sel, series, held, box, root, total, peaks, peaks_in,
    load_sem, beam_send, beam_recv, band_send, band_recv, peak_send, peak_recv,
):
    me = lax.axis_index("beam")
    band = lax.axis_index("band")
    column = me // RING
    place = lax.rem(me, RING)

    band_x, band_y, core = band // 8, lax.rem(band // 2, 4), lax.rem(band, 2)
    band_peers = [
        lax.rem(band_x + x, 2) * 8 + lax.rem(band_y + y, 4) * 2 + lax.rem(core + c, 2)
        for x, y in ((1, 2), (1, 1), (1, 3), (0, 2), (1, 0), (0, 1), (0, 3), (0, 0))
        for c in (0, 1)
        if x or y or c
    ]

    barrier = pltpu.get_barrier_semaphore()

    def greet_beam(i, _):
        step = i // 2
        there = jnp.where(lax.rem(step, 2) == 1, (step + 1) // 2, lax.rem(RING - step // 2, RING))
        peer = lax.rem(column + lax.rem(i, 2), 2) * RING + there

        @pl.when(peer != me)
        def _():
            pl.semaphore_signal(barrier, inc=1, device_id=(peer, band), device_id_type=MESH)

        return 0

    lax.fori_loop(0, BEAMS, greet_beam, 0)

    def greet_band(i, _):
        pl.semaphore_signal(barrier, inc=1, device_id=(me, lax.rem(band + i, BANDS)), device_id_type=MESH)
        return 0

    lax.fori_loop(1, BANDS, greet_band, 0)

    loads = [
        pltpu.make_async_copy(x_hbm.at[:, :, pl.ds(h * LANES, LANES)], x_ref.at[h], load_sem.at[h]) for h in range(HALVES)
    ] + [
        pltpu.make_async_copy(chan_hbm, chan_ref, load_sem.at[2]),
        pltpu.make_async_copy(shift_hbm.at[pl.ds(band * OWN, OWN)], shift_own, load_sem.at[3]),
        pltpu.make_async_copy(width_hbm, width_ref, load_sem.at[4]),
    ]
    for load in loads:
        load.start()

    def gather(h):
        loads[h].wait()

        def widen(i, _):
            rows = pl.ds(pl.multiple_of(i * 8 * BEAMS, 8 * BEAMS), 8 * BEAMS)
            wide[h, rows, :] = x_ref[h, pl.ds(i * 8, 8)].astype(F32).reshape(8 * BEAMS, LANES)
            return 0

        lax.fori_loop(0, SAMPLES // 8, widen, 0)

        def pick(b, _):
            block[h, b] = wide.at[h][pl.ds(b, SAMPLES, stride=BEAMS), :].astype(BF16)
            return 0

        lax.fori_loop(0, BEAMS, pick, 0, unroll=4)
        got[h, me] = block[h, me]

    gather(0)
    pl.semaphore_wait(barrier, BEAMS - 1 + BANDS - 1)

    def send_beams(h, other):
        def send(i, _):
            peer = lax.rem(column + other, 2) * RING + lax.rem(place + i, RING)
            pltpu.make_async_remote_copy(
                src_ref=block.at[h, peer], dst_ref=got.at[h, me],
                send_sem=beam_send.at[h], recv_sem=beam_recv.at[h, other],
                device_id=(peer, band), device_id_type=MESH,
            ).start()
            return 0

        lax.fori_loop(1 - other, RING, send, 0)

    send_beams(0, 0)
    send_beams(0, 1)
    gather(1)
    send_beams(1, 0)
    send_beams(1, 1)

    loads[2].wait()
    loads[3].wait()
    loads[4].wait()

    row = lax.broadcasted_iota(jnp.int32, (GROUPS * 8, LANES), 0)
    lane = lax.broadcasted_iota(jnp.int32, (GROUPS * 8, LANES), 1)
    mine = lax.rem(row, 8) == lane // 16
    for h in range(HALVES):
        delays = chan_ref[:, h * LANES : (h + 1) * LANES]
        delays = jnp.broadcast_to(delays[:, None, :], (GROUPS, 8, LANES)).reshape(GROUPS * 8, LANES)
        for k in range(2):
            chan_sel[h, :, k * LANES : (k + 1) * LANES] = jnp.where(mine & (delays == k), 1.0, 0.0).astype(BF16)

    col = lax.broadcasted_iota(jnp.int32, (32, 256), 1)
    high = lax.rem(col // 8, 2) == 1
    for h in range(HALVES):
        first, second = shift_own[0:32, :], shift_own[32:64, :]
        if h == 0:
            second = pltpu.roll(second, 8, 1)
        else:
            first = pltpu.roll(first, 256 - 8, 1)
        for k in range(SHIFTS):
            shift_sel[h, k * OWN : k * OWN + 32, :] = jnp.where((first == k) & jnp.logical_not(high), 1.0, 0.0).astype(BF16)
            shift_sel[h, k * OWN + 32 : (k + 1) * OWN, :] = jnp.where((second == k) & high, 1.0, 0.0).astype(BF16)

    lag = (
        lax.broadcasted_iota(jnp.int32, (256, LANES), 1) + LANES
        - lax.broadcasted_iota(jnp.int32, (256, LANES), 0)
    )
    which = lax.broadcasted_iota(jnp.int32, (8, LANES), 1)
    scale = jnp.ones((8, LANES), F32)
    for i in range(NBOX):
        width = width_ref[i]
        box[:, i * LANES : (i + 1) * LANES] = jnp.where((lag >= 0) & (lag < width), 1.0, 0.0).astype(BF16)
        scale = jnp.where(which == i, width.astype(F32), scale)
    root[...] = jnp.sqrt(scale)

    total[...] = jnp.zeros_like(total)

    def arrived(buffer, sem):
        pltpu.make_async_copy(buffer, buffer, sem).wait()

    def tiles_of(h, side):
        return got[h, side * RING : (side + 1) * RING].astype(F32).reshape(RING * SAMPLES, LANES).astype(BF16)

    def channel_sum(h, now, later):
        return dot_t(chan_sel[h], jnp.concatenate([now, later], axis=1)).astype(BF16)

    def keep(h, first, summed):
        for i in range(summed.shape[1] // LANES):
            series[h, :, first + i] = summed[:, i * LANES : (i + 1) * LANES].reshape(BANDS, SUB_ROWS, LANES)

    def inner_tiles(h, side):
        data = got[h, pl.ds(side * RING, RING)].astype(F32).reshape(RING * SAMPLES, LANES).astype(BF16)
        keep(h, 5 * side, channel_sum(h, data[: 4 * LANES], data[LANES:]))

    def send_series(h, part, first, count):
        for peer in band_peers:
            pltpu.make_async_remote_copy(
                src_ref=series.at[h, peer, pl.ds(first, count)], dst_ref=held.at[h, band, pl.ds(first, count)],
                send_sem=band_send.at[h], recv_sem=band_recv.at[h, part],
                device_id=(me, peer), device_id_type=MESH,
            ).start()
        held[h, band, pl.ds(first, count)] = series[h, band, pl.ds(first, count)]

    def subseries(h):
        arrived(got.at[h, pl.ds(0, RING - 1)], beam_recv.at[h, 0])
        inner_tiles(h, column)
        send_series(h, 0, 5 * column, 4)
        arrived(got.at[h, pl.ds(0, RING)], beam_recv.at[h, 1])
        inner_tiles(h, 1 - column)
        keep(h, 4, channel_sum(h, tiles_of(h, 0)[4 * LANES :], tiles_of(h, 1)[:LANES]))
        send_series(h, 1, 4 * (1 - column), 5)

    def trials(h):
        arrived(held.at[h, pl.ds(0, BANDS - 1), pl.ds(0, 4)], band_recv.at[h, 0])
        arrived(held.at[h, pl.ds(0, BANDS - 1), pl.ds(0, 5)], band_recv.at[h, 1])
        for tile in range(0, TILES_MID, 2):
            tiles = [t for t in (tile, tile + 1) if t < TILES_MID]
            low = max(0, tiles[0] - TILES_OUT + 1)
            top = min(SHIFTS - 1, tiles[-1])
            data = jnp.concatenate([held[h, :, t].reshape(BANDS * SUB_ROWS, LANES) for t in tiles], axis=1)
            part = dot(shift_sel[h, low * OWN : (top + 1) * OWN, :], data)
            for n, t in enumerate(tiles):
                for k in range(low, top + 1):
                    o = t - k
                    if 0 <= o < TILES_OUT:
                        total[:, o * LANES : (o + 1) * LANES] += part[
                            (k - low) * OWN : (k - low + 1) * OWN, n * LANES : (n + 1) * LANES
                        ]

    subseries(0)
    trials(0)
    subseries(1)
    trials(1)

    dm = (total[...] * (1.0 / 64.0)).astype(BF16)
    dm_ref[...] = dm
    values = dm.astype(F32)
    centre = jnp.mean(values, axis=1, keepdims=True)
    off = values - centre
    spread = jnp.mean(off * off, axis=1, keepdims=True)
    normed = (off / jnp.sqrt(spread + EPSILON)).astype(BF16)
    before = jnp.concatenate([jnp.zeros((OWN, LANES), BF16), normed[:, : 3 * LANES]], axis=1)
    pairs = jnp.concatenate(
        [
            jnp.concatenate([before[:, k * LANES : (k + 1) * LANES], normed[:, k * LANES : (k + 1) * LANES]], axis=1)
            for k in range(TILES_OUT)
        ],
        axis=0,
    )
    best = [[] for _ in range(TILES_OUT)]
    for i in range(0, NBOX, 2):
        sums = dot(pairs, box[:, i * LANES : (i + 2) * LANES])
        for k in range(TILES_OUT):
            top = jnp.max(sums[k * OWN : (k + 1) * OWN].reshape(8, 8, 2 * LANES), axis=0)
            best[k] += [top[:, :LANES], top[:, LANES:]]
    rows = jnp.concatenate([jnp.max(jnp.stack(best[k], axis=0), axis=1) for k in range(TILES_OUT)] * 2, axis=0)
    found = jnp.max(rows.T, axis=0, keepdims=True)
    found = jnp.concatenate([found if k == 0 else pltpu.roll(found, LANES - k * NBOX, 1) for k in range(TILES_OUT)] * 2, axis=0)
    peaks[...] = found / root[...]

    for peer in band_peers:
        pltpu.make_async_remote_copy(
            src_ref=peaks, dst_ref=peaks_in.at[band],
            send_sem=peak_send, recv_sem=peak_recv,
            device_id=(me, peer), device_id_type=MESH,
        ).start()
    peaks_in[band] = peaks[...]
    for h in range(HALVES):
        arrived(block.at[h, pl.ds(0, BEAMS - 1)], beam_send.at[h])
        arrived(series.at[h, pl.ds(0, BANDS - 1)], band_send.at[h])
    arrived(peaks_in.at[pl.ds(0, BANDS - 1)], peak_recv)
    peak_ref[...] = jnp.max(peaks_in[...], axis=0)[:TILES_OUT, :NBOX]
    arrived(peaks_in.at[pl.ds(0, BANDS - 1)], peak_send)


def local(intensity, chan_shift, sub_shift, widths):
    vmem = pl.BlockSpec(memory_space=pltpu.VMEM)
    operands = [pltpu.with_memory_space_constraint(a, pltpu.HBM) for a in (intensity, chan_shift, sub_shift, widths)]
    dm, peak = pl.pallas_call(
        kernel,
        out_shape=(
            jax.ShapeDtypeStruct((OWN, TILES_OUT * LANES), BF16),
            jax.ShapeDtypeStruct((TILES_OUT, NBOX), F32),
        ),
        in_specs=[pl.BlockSpec(memory_space=pltpu.HBM)] * 4,
        out_specs=(vmem, vmem),
        scratch_shapes=[
            pltpu.VMEM((HALVES, SAMPLES, BEAMS, LANES), BF16),
            pltpu.VMEM((GROUPS, 2 * LANES), jnp.int32),
            pltpu.SMEM((NBOX,), jnp.int32),
            pltpu.VMEM((HALVES, SAMPLES * BEAMS, LANES), F32),
            pltpu.VMEM((HALVES, BEAMS, SAMPLES, LANES), BF16),
            pltpu.VMEM((HALVES, BEAMS, SAMPLES, LANES), BF16),
            pltpu.VMEM((HALVES, GROUPS * 8, 2 * LANES), BF16),
            pltpu.VMEM((OWN, 256), jnp.int32),
            pltpu.VMEM((HALVES, SHIFTS * OWN, 256), BF16),
            pltpu.VMEM((HALVES, BANDS, TILES_MID, SUB_ROWS, LANES), BF16),
            pltpu.VMEM((HALVES, BANDS, TILES_MID, SUB_ROWS, LANES), BF16),
            pltpu.VMEM((256, NBOX * LANES), BF16),
            pltpu.VMEM((8, LANES), F32),
            pltpu.VMEM((OWN, TILES_OUT * LANES), F32),
            pltpu.VMEM((8, LANES), F32),
            pltpu.VMEM((BANDS, 8, LANES), F32),
            pltpu.SemaphoreType.DMA((5,)),
            pltpu.SemaphoreType.DMA((HALVES,)),
            pltpu.SemaphoreType.DMA((HALVES, 2)),
            pltpu.SemaphoreType.DMA((HALVES,)),
            pltpu.SemaphoreType.DMA((HALVES, 2)),
            pltpu.SemaphoreType.DMA,
            pltpu.SemaphoreType.DMA,
        ],
        compiler_params=pltpu.CompilerParams(
            collective_id=0, has_side_effects=True, vmem_limit_bytes=48 << 20
        ),
        cost_estimate=pl.CostEstimate(flops=4_000_000_000, bytes_accessed=2_000_000, transcendentals=0),
    )(*operands)
    return dm.reshape(OWN, 1, TILES_OUT * LANES), peak.T.reshape(1, NBOX, TILES_OUT)


def solution(mesh):
    return jax.shard_map(
        local,
        mesh=mesh,
        in_specs=(P("beam", None, "band"), P(None, "band"), P(), P()),
        out_specs=(P("band", "beam", None), P("beam", None, None)),
        check_vma=False,
    )
```

```python
import jax
import jax.numpy as jnp
from jax import lax
from jax.experimental import pallas as pl
from jax.experimental.pallas import tpu as pltpu
from jax.sharding import PartitionSpec as P

MESH = pl.DeviceIdType.MESH
F32 = jnp.float32
BF16 = jnp.bfloat16
LANES = 128
SAMPLES = 40
BEAMS = 32
RING = 16
BANDS = 16
HALVES = 2
GROUPS = 32
SUB_ROWS = 16
TILES_IN = 10
TILES_MID = 9
TILES_OUT = 4
SHIFTS = 6
OWN = 64
NBOX = 16
EPSILON = 1e-05


def dot(a, b):
    return lax.dot_general(a, b, (((1,), (0,)), ((), ())), preferred_element_type=F32)


def dot_t(a, b):
    return lax.dot_general(a, b, (((1,), (1,)), ((), ())), preferred_element_type=F32)


def kernel(
    x_hbm, chan_hbm, shift_hbm, width_hbm, dm_ref, peak_ref,
    x_ref, chan_ref, width_ref, wide, block, got, chan_sel, shift_own, shift_sel, series, held, box, root, total, peaks, peaks_in,
    load_sem, beam_send, beam_recv, band_send, band_recv, peak_send, peak_recv,
):
    me = lax.axis_index("beam")
    band = lax.axis_index("band")
    column = me // RING
    place = lax.rem(me, RING)

    band_x, band_y, core = band // 8, lax.rem(band // 2, 4), lax.rem(band, 2)
    band_peers = [
        lax.rem(band_x + x, 2) * 8 + lax.rem(band_y + y, 4) * 2 + lax.rem(core + c, 2)
        for x, y in ((1, 2), (1, 1), (1, 3), (0, 2), (1, 0), (0, 1), (0, 3), (0, 0))
        for c in (0, 1)
        if x or y or c
    ]

    barrier = pltpu.get_barrier_semaphore()

    def greet_beam(i, _):
        step = i // 2
        there = jnp.where(lax.rem(step, 2) == 1, (step + 1) // 2, lax.rem(RING - step // 2, RING))
        peer = lax.rem(column + lax.rem(i, 2), 2) * RING + there

        @pl.when(peer != me)
        def _():
            pl.semaphore_signal(barrier, inc=1, device_id=(peer, band), device_id_type=MESH)

        return 0

    lax.fori_loop(0, BEAMS, greet_beam, 0)

    def greet_band(i, _):
        pl.semaphore_signal(barrier, inc=1, device_id=(me, lax.rem(band + i, BANDS)), device_id_type=MESH)
        return 0

    lax.fori_loop(1, BANDS, greet_band, 0)

    loads = [
        pltpu.make_async_copy(x_hbm.at[:, :, pl.ds(h * LANES, LANES)], x_ref.at[h], load_sem.at[h]) for h in range(HALVES)
    ] + [
        pltpu.make_async_copy(chan_hbm, chan_ref, load_sem.at[2]),
        pltpu.make_async_copy(shift_hbm.at[pl.ds(band * OWN, OWN)], shift_own, load_sem.at[3]),
        pltpu.make_async_copy(width_hbm, width_ref, load_sem.at[4]),
    ]
    for load in loads:
        load.start()

    def gather(h):
        loads[h].wait()

        def widen(i, _):
            rows = pl.ds(pl.multiple_of(i * 8 * BEAMS, 8 * BEAMS), 8 * BEAMS)
            wide[h, rows, :] = x_ref[h, pl.ds(i * 8, 8)].astype(F32).reshape(8 * BEAMS, LANES)
            return 0

        lax.fori_loop(0, SAMPLES // 8, widen, 0)

        def pick(b, _):
            block[h, b] = wide.at[h][pl.ds(b, SAMPLES, stride=BEAMS), :].astype(BF16)
            return 0

        lax.fori_loop(0, BEAMS, pick, 0, unroll=4)
        got[h, me] = block[h, me]

    gather(0)
    pl.semaphore_wait(barrier, BEAMS - 1 + BANDS - 1)

    def send_block(h, own, step):
        peer = lax.rem(column + 1 - own, 2) * RING + lax.rem(place + step + RING, RING)
        pltpu.make_async_remote_copy(
            src_ref=block.at[h, peer], dst_ref=got.at[h, me],
            send_sem=beam_send.at[h], recv_sem=beam_recv.at[h, own],
            device_id=(peer, band), device_id_type=MESH,
        ).start()

    def send_beams(h, own):
        def send(i, _):
            skip = lax.rem(RING - place, RING)
            step = i if h == 0 else jnp.where(i == own, skip, jnp.where(i <= skip, i - 1, i))
            if h == 1 and own:
                step = jnp.where(place == 0, i, step)
            send_block(h, own, step)
            return 0

        lax.fori_loop(own, RING, send, 0)

    send_beams(0, 0)
    send_beams(0, 1)
    gather(1)
    send_beams(1, 0)
    send_beams(1, 1)

    loads[2].wait()
    loads[3].wait()
    loads[4].wait()

    row = lax.broadcasted_iota(jnp.int32, (GROUPS * 8, LANES), 0)
    lane = lax.broadcasted_iota(jnp.int32, (GROUPS * 8, LANES), 1)
    mine = lax.rem(row, 8) == lane // 16
    for h in range(HALVES):
        delays = chan_ref[:, h * LANES : (h + 1) * LANES]
        delays = jnp.broadcast_to(delays[:, None, :], (GROUPS, 8, LANES)).reshape(GROUPS * 8, LANES)
        for k in range(2):
            chan_sel[h, :, k * LANES : (k + 1) * LANES] = jnp.where(mine & (delays == k), 1.0, 0.0).astype(BF16)

    col = lax.broadcasted_iota(jnp.int32, (32, 256), 1)
    high = lax.rem(col // 8, 2) == 1
    for h in range(HALVES):
        first, second = shift_own[0:32, :], shift_own[32:64, :]
        if h == 0:
            second = pltpu.roll(second, 8, 1)
        else:
            first = pltpu.roll(first, 256 - 8, 1)
        for k in range(SHIFTS):
            shift_sel[h, k * OWN : k * OWN + 32, :] = jnp.where((first == k) & jnp.logical_not(high), 1.0, 0.0).astype(BF16)
            shift_sel[h, k * OWN + 32 : (k + 1) * OWN, :] = jnp.where((second == k) & high, 1.0, 0.0).astype(BF16)

    lag = (
        lax.broadcasted_iota(jnp.int32, (256, LANES), 1) + LANES
        - lax.broadcasted_iota(jnp.int32, (256, LANES), 0)
    )
    which = lax.broadcasted_iota(jnp.int32, (8, LANES), 1)
    scale = jnp.ones((8, LANES), F32)
    for i in range(NBOX):
        width = width_ref[i]
        box[:, i * LANES : (i + 1) * LANES] = jnp.where((lag >= 0) & (lag < width), 1.0, 0.0).astype(BF16)
        scale = jnp.where(which == i, width.astype(F32), scale)
    root[...] = jnp.sqrt(scale)

    total[...] = jnp.zeros_like(total)

    def arrived(buffer, sem):
        pltpu.make_async_copy(buffer, buffer, sem).wait()

    def tiles_of(h, side):
        return got[h, side * RING : (side + 1) * RING].astype(F32).reshape(RING * SAMPLES, LANES).astype(BF16)

    def channel_sum(h, now, later):
        return dot_t(chan_sel[h], jnp.concatenate([now, later], axis=1)).astype(BF16)

    def keep(h, first, summed):
        for i in range(summed.shape[1] // LANES):
            series[h, :, first + i] = summed[:, i * LANES : (i + 1) * LANES].reshape(BANDS, SUB_ROWS, LANES)

    def inner_tiles(h, side):
        data = got[h, pl.ds(side * RING, RING)].astype(F32).reshape(RING * SAMPLES, LANES).astype(BF16)
        keep(h, 5 * side, channel_sum(h, data[: 4 * LANES], data[LANES:]))

    def send_series(h, part, first, count):
        for peer in band_peers:
            pltpu.make_async_remote_copy(
                src_ref=series.at[h, peer, pl.ds(first, count)], dst_ref=held.at[h, band, pl.ds(first, count)],
                send_sem=band_send.at[h], recv_sem=band_recv.at[h, part],
                device_id=(me, peer), device_id_type=MESH,
            ).start()
        held[h, band, pl.ds(first, count)] = series[h, band, pl.ds(first, count)]

    def subseries(h, last):
        side = column if last else 1 - column
        arrived(got.at[h, pl.ds(0, RING - last)], beam_recv.at[h, last])
        inner_tiles(h, side)
        if last:
            keep(h, 4, channel_sum(h, tiles_of(h, 0)[4 * LANES :], tiles_of(h, 1)[:LANES]))
            send_series(h, 1, 4 * side, 5)
        else:
            send_series(h, 0, 5 * side, 4)

    def trials(h):
        arrived(held.at[h, pl.ds(0, BANDS - 1), pl.ds(0, 4)], band_recv.at[h, 0])
        arrived(held.at[h, pl.ds(0, BANDS - 1), pl.ds(0, 5)], band_recv.at[h, 1])
        for tile in range(0, TILES_MID, 2):
            tiles = [t for t in (tile, tile + 1) if t < TILES_MID]
            low = max(0, tiles[0] - TILES_OUT + 1)
            top = min(SHIFTS - 1, tiles[-1])
            data = jnp.concatenate([held[h, :, t].reshape(BANDS * SUB_ROWS, LANES) for t in tiles], axis=1)
            part = dot(shift_sel[h, low * OWN : (top + 1) * OWN, :], data)
            for n, t in enumerate(tiles):
                for k in range(low, top + 1):
                    o = t - k
                    if 0 <= o < TILES_OUT:
                        total[:, o * LANES : (o + 1) * LANES] += part[
                            (k - low) * OWN : (k - low + 1) * OWN, n * LANES : (n + 1) * LANES
                        ]

    subseries(0, 0)
    subseries(0, 1)
    trials(0)
    subseries(1, 0)
    subseries(1, 1)
    trials(1)

    dm = (total[...] * (1.0 / 64.0)).astype(BF16)
    dm_ref[...] = dm
    values = dm.astype(F32)
    centre = jnp.mean(values, axis=1, keepdims=True)
    off = values - centre
    spread = jnp.mean(off * off, axis=1, keepdims=True)
    normed = (off / jnp.sqrt(spread + EPSILON)).astype(BF16)
    before = jnp.concatenate([jnp.zeros((OWN, LANES), BF16), normed[:, : 3 * LANES]], axis=1)
    pairs = jnp.concatenate(
        [
            jnp.concatenate([before[:, k * LANES : (k + 1) * LANES], normed[:, k * LANES : (k + 1) * LANES]], axis=1)
            for k in range(TILES_OUT)
        ],
        axis=0,
    )
    best = [[] for _ in range(TILES_OUT)]
    for i in range(0, NBOX, 2):
        sums = dot(pairs, box[:, i * LANES : (i + 2) * LANES])
        for k in range(TILES_OUT):
            top = jnp.max(sums[k * OWN : (k + 1) * OWN].reshape(8, 8, 2 * LANES), axis=0)
            best[k] += [top[:, :LANES], top[:, LANES:]]
    rows = jnp.concatenate([jnp.max(jnp.stack(best[k], axis=0), axis=1) for k in range(TILES_OUT)] * 2, axis=0)
    found = jnp.max(rows.T, axis=0, keepdims=True)
    found = jnp.concatenate([found if k == 0 else pltpu.roll(found, LANES - k * NBOX, 1) for k in range(TILES_OUT)] * 2, axis=0)
    peaks[...] = found / root[...]

    for peer in band_peers:
        pltpu.make_async_remote_copy(
            src_ref=peaks, dst_ref=peaks_in.at[band],
            send_sem=peak_send, recv_sem=peak_recv,
            device_id=(me, peer), device_id_type=MESH,
        ).start()
    peaks_in[band] = peaks[...]
    for h in range(HALVES):
        arrived(block.at[h, pl.ds(0, BEAMS - 1)], beam_send.at[h])
        arrived(series.at[h, pl.ds(0, BANDS - 1)], band_send.at[h])
    arrived(peaks_in.at[pl.ds(0, BANDS - 1)], peak_recv)
    peak_ref[...] = jnp.max(peaks_in[...], axis=0)[:TILES_OUT, :NBOX]
    arrived(peaks_in.at[pl.ds(0, BANDS - 1)], peak_send)


def local(intensity, chan_shift, sub_shift, widths):
    vmem = pl.BlockSpec(memory_space=pltpu.VMEM)
    operands = [pltpu.with_memory_space_constraint(a, pltpu.HBM) for a in (intensity, chan_shift, sub_shift, widths)]
    dm, peak = pl.pallas_call(
        kernel,
        out_shape=(
            jax.ShapeDtypeStruct((OWN, TILES_OUT * LANES), BF16),
            jax.ShapeDtypeStruct((TILES_OUT, NBOX), F32),
        ),
        in_specs=[pl.BlockSpec(memory_space=pltpu.HBM)] * 4,
        out_specs=(vmem, vmem),
        scratch_shapes=[
            pltpu.VMEM((HALVES, SAMPLES, BEAMS, LANES), BF16),
            pltpu.VMEM((GROUPS, 2 * LANES), jnp.int32),
            pltpu.SMEM((NBOX,), jnp.int32),
            pltpu.VMEM((HALVES, SAMPLES * BEAMS, LANES), F32),
            pltpu.VMEM((HALVES, BEAMS, SAMPLES, LANES), BF16),
            pltpu.VMEM((HALVES, BEAMS, SAMPLES, LANES), BF16),
            pltpu.VMEM((HALVES, GROUPS * 8, 2 * LANES), BF16),
            pltpu.VMEM((OWN, 256), jnp.int32),
            pltpu.VMEM((HALVES, SHIFTS * OWN, 256), BF16),
            pltpu.VMEM((HALVES, BANDS, TILES_MID, SUB_ROWS, LANES), BF16),
            pltpu.VMEM((HALVES, BANDS, TILES_MID, SUB_ROWS, LANES), BF16),
            pltpu.VMEM((256, NBOX * LANES), BF16),
            pltpu.VMEM((8, LANES), F32),
            pltpu.VMEM((OWN, TILES_OUT * LANES), F32),
            pltpu.VMEM((8, LANES), F32),
            pltpu.VMEM((BANDS, 8, LANES), F32),
            pltpu.SemaphoreType.DMA((5,)),
            pltpu.SemaphoreType.DMA((HALVES,)),
            pltpu.SemaphoreType.DMA((HALVES, 2)),
            pltpu.SemaphoreType.DMA((HALVES,)),
            pltpu.SemaphoreType.DMA((HALVES, 2)),
            pltpu.SemaphoreType.DMA,
            pltpu.SemaphoreType.DMA,
        ],
        compiler_params=pltpu.CompilerParams(
            collective_id=0, has_side_effects=True, vmem_limit_bytes=48 << 20
        ),
        cost_estimate=pl.CostEstimate(flops=4_000_000_000, bytes_accessed=2_000_000, transcendentals=0),
    )(*operands)
    return dm.reshape(OWN, 1, TILES_OUT * LANES), peak.T.reshape(1, NBOX, TILES_OUT)


def solution(mesh):
    return jax.shard_map(
        local,
        mesh=mesh,
        in_specs=(P("beam", None, "band"), P(None, "band"), P(), P()),
        out_specs=(P("band", "beam", None), P("beam", None, None)),
        check_vma=False,
    )
```

```python
import jax
import jax.numpy as jnp
from jax import lax
from jax.experimental import pallas as pl
from jax.experimental.pallas import tpu as pltpu
from jax.sharding import PartitionSpec as P

MESH = pl.DeviceIdType.MESH
F32 = jnp.float32
BF16 = jnp.bfloat16
LANES = 128
SAMPLES = 40
BEAMS = 32
RING = 16
BANDS = 16
HALVES = 2
GROUPS = 32
SUB_ROWS = 16
TILES_IN = 10
TILES_MID = 9
TILES_OUT = 4
SHIFTS = 6
OWN = 64
NBOX = 16
EPSILON = 1e-05


def dot(a, b):
    return lax.dot_general(a, b, (((1,), (0,)), ((), ())), preferred_element_type=F32)


def dot_t(a, b):
    return lax.dot_general(a, b, (((1,), (1,)), ((), ())), preferred_element_type=F32)


def kernel(
    x_hbm, chan_hbm, shift_hbm, width_hbm, dm_ref, peak_ref,
    x_ref, chan_ref, width_ref, wide, block, got, chan_sel, shift_own, shift_sel, series, held, box, root, total, peaks, peaks_in,
    load_sem, ready, beam_send, beam_recv, band_send, band_recv, peak_send, peak_recv,
):
    me = lax.axis_index("beam")
    band = lax.axis_index("band")
    column = me // RING
    place = lax.rem(me, RING)

    band_x, band_y, core = band // 8, lax.rem(band // 2, 4), lax.rem(band, 2)
    band_peers = [
        lax.rem(band_x + x, 2) * 8 + lax.rem(band_y + y, 4) * 2 + lax.rem(core + c, 2)
        for x, y in ((1, 2), (1, 1), (1, 3), (0, 2), (1, 0), (0, 1), (0, 3), (0, 0))
        for c in (0, 1)
        if x or y or c
    ]

    barrier = pltpu.get_barrier_semaphore()

    def greet_beam(i, _):
        there = jnp.where(lax.rem(i, 2) == 1, (i + 1) // 2, lax.rem(RING - i // 2, RING))

        @pl.when(there != place)
        def _():
            pl.semaphore_signal(barrier, inc=1, device_id=(column * RING + there, band), device_id_type=MESH)

        @pl.when(column == 0)
        def _():
            pl.semaphore_signal(barrier, inc=1, device_id=(RING + there, band), device_id_type=MESH)

        return 0

    lax.fori_loop(0, RING, greet_beam, 0)

    def greet_band(i, _):
        pl.semaphore_signal(barrier, inc=1, device_id=(me, lax.rem(band + i, BANDS)), device_id_type=MESH)
        return 0

    lax.fori_loop(1, BANDS, greet_band, 0)

    loads = [
        pltpu.make_async_copy(x_hbm.at[:, :, pl.ds(h * LANES, LANES)], x_ref.at[h], load_sem.at[h]) for h in range(HALVES)
    ] + [
        pltpu.make_async_copy(chan_hbm, chan_ref, load_sem.at[2]),
        pltpu.make_async_copy(shift_hbm.at[pl.ds(band * OWN, OWN)], shift_own, load_sem.at[3]),
        pltpu.make_async_copy(width_hbm, width_ref, load_sem.at[4]),
    ]
    for load in loads:
        load.start()

    def gather(h):
        loads[h].wait()

        def widen(i, _):
            rows = pl.ds(pl.multiple_of(i * 8 * BEAMS, 8 * BEAMS), 8 * BEAMS)
            wide[h, rows, :] = x_ref[h, pl.ds(i * 8, 8)].astype(F32).reshape(8 * BEAMS, LANES)
            return 0

        lax.fori_loop(0, SAMPLES // 8, widen, 0)

        def pick(b, _):
            block[h, b] = wide.at[h][pl.ds(b, SAMPLES, stride=BEAMS), :].astype(BF16)
            return 0

        lax.fori_loop(0, BEAMS, pick, 0, unroll=4)
        got[h, me] = block[h, me]

    gather(0)
    pl.semaphore_wait(barrier, jnp.where(column == 0, RING, BEAMS) - 1 + BANDS - 1)

    @pl.when(column == 1)
    def _():
        pl.semaphore_signal(ready, inc=1, device_id=(place, band), device_id_type=MESH)


    def send_block(h, own, step):
        peer = lax.rem(column + 1 - own, 2) * RING + lax.rem(place + step + RING, RING)
        pltpu.make_async_remote_copy(
            src_ref=block.at[h, peer], dst_ref=got.at[h, me],
            send_sem=beam_send.at[h], recv_sem=beam_recv.at[h, own],
            device_id=(peer, band), device_id_type=MESH,
        ).start()

    def send_beams(h, own):
        def send(i, _):
            skip = lax.rem(RING - place, RING)
            step = i if h == 0 else jnp.where(i == own, skip, jnp.where(i <= skip, i - 1, i))
            if h == 1 and own:
                step = jnp.where(place == 0, i, step)
            send_block(h, own, step)
            return 0

        lax.fori_loop(own, RING, send, 0)

    send_beams(0, 1)
    gather(1)

    @pl.when(column == 0)
    def _():
        pl.semaphore_wait(ready, 1)

    send_beams(0, 0)
    send_beams(1, 0)

    loads[2].wait()
    loads[3].wait()
    loads[4].wait()

    row = lax.broadcasted_iota(jnp.int32, (GROUPS * 8, LANES), 0)
    lane = lax.broadcasted_iota(jnp.int32, (GROUPS * 8, LANES), 1)
    mine = lax.rem(row, 8) == lane // 16
    for h in range(HALVES):
        delays = chan_ref[:, h * LANES : (h + 1) * LANES]
        delays = jnp.broadcast_to(delays[:, None, :], (GROUPS, 8, LANES)).reshape(GROUPS * 8, LANES)
        for k in range(2):
            chan_sel[h, :, k * LANES : (k + 1) * LANES] = jnp.where(mine & (delays == k), 1.0, 0.0).astype(BF16)

    col = lax.broadcasted_iota(jnp.int32, (32, 256), 1)
    high = lax.rem(col // 8, 2) == 1
    for h in range(HALVES):
        first, second = shift_own[0:32, :], shift_own[32:64, :]
        if h == 0:
            second = pltpu.roll(second, 8, 1)
        else:
            first = pltpu.roll(first, 256 - 8, 1)
        for k in range(SHIFTS):
            shift_sel[h, k * OWN : k * OWN + 32, :] = jnp.where((first == k) & jnp.logical_not(high), 1.0, 0.0).astype(BF16)
            shift_sel[h, k * OWN + 32 : (k + 1) * OWN, :] = jnp.where((second == k) & high, 1.0, 0.0).astype(BF16)

    lag = (
        lax.broadcasted_iota(jnp.int32, (256, LANES), 1) + LANES
        - lax.broadcasted_iota(jnp.int32, (256, LANES), 0)
    )
    which = lax.broadcasted_iota(jnp.int32, (8, LANES), 1)
    scale = jnp.ones((8, LANES), F32)
    for i in range(NBOX):
        width = width_ref[i]
        box[:, i * LANES : (i + 1) * LANES] = jnp.where((lag >= 0) & (lag < width), 1.0, 0.0).astype(BF16)
        scale = jnp.where(which == i, width.astype(F32), scale)
    root[...] = jnp.sqrt(scale)

    total[...] = jnp.zeros_like(total)

    def arrived(buffer, sem):
        pltpu.make_async_copy(buffer, buffer, sem).wait()

    def tiles_of(h, side):
        return got[h, side * RING : (side + 1) * RING].astype(F32).reshape(RING * SAMPLES, LANES).astype(BF16)

    def channel_sum(h, now, later):
        return dot_t(chan_sel[h], jnp.concatenate([now, later], axis=1)).astype(BF16)

    def keep(h, first, summed):
        for i in range(summed.shape[1] // LANES):
            series[h, :, first + i] = summed[:, i * LANES : (i + 1) * LANES].reshape(BANDS, SUB_ROWS, LANES)

    def inner_tiles(h, side):
        data = got[h, pl.ds(side * RING, RING)].astype(F32).reshape(RING * SAMPLES, LANES).astype(BF16)
        keep(h, 5 * side, channel_sum(h, data[: 4 * LANES], data[LANES:]))

    def send_series(h, part, first, count):
        for peer in band_peers:
            pltpu.make_async_remote_copy(
                src_ref=series.at[h, peer, pl.ds(first, count)], dst_ref=held.at[h, band, pl.ds(first, count)],
                send_sem=band_send.at[h], recv_sem=band_recv.at[h, part],
                device_id=(me, peer), device_id_type=MESH,
            ).start()
        held[h, band, pl.ds(first, count)] = series[h, band, pl.ds(first, count)]

    def subseries(h, own, last):
        side = column if own else 1 - column
        arrived(got.at[h, pl.ds(0, RING - own)], beam_recv.at[h, own])
        inner_tiles(h, side)
        if last:
            keep(h, 4, channel_sum(h, tiles_of(h, 0)[4 * LANES :], tiles_of(h, 1)[:LANES]))
            send_series(h, 1, 4 * side, 5)
        else:
            send_series(h, 0, 5 * side, 4)

    def trials(h):
        arrived(held.at[h, pl.ds(0, BANDS - 1), pl.ds(0, 4)], band_recv.at[h, 0])
        arrived(held.at[h, pl.ds(0, BANDS - 1), pl.ds(0, 5)], band_recv.at[h, 1])
        for tile in range(0, TILES_MID, 2):
            tiles = [t for t in (tile, tile + 1) if t < TILES_MID]
            low = max(0, tiles[0] - TILES_OUT + 1)
            top = min(SHIFTS - 1, tiles[-1])
            data = jnp.concatenate([held[h, :, t].reshape(BANDS * SUB_ROWS, LANES) for t in tiles], axis=1)
            part = dot(shift_sel[h, low * OWN : (top + 1) * OWN, :], data)
            for n, t in enumerate(tiles):
                for k in range(low, top + 1):
                    o = t - k
                    if 0 <= o < TILES_OUT:
                        total[:, o * LANES : (o + 1) * LANES] += part[
                            (k - low) * OWN : (k - low + 1) * OWN, n * LANES : (n + 1) * LANES
                        ]

    subseries(0, 1, False)
    send_beams(1, 1)
    subseries(0, 0, True)
    trials(0)
    subseries(1, 0, False)
    subseries(1, 1, True)
    trials(1)

    dm = (total[...] * (1.0 / 64.0)).astype(BF16)
    dm_ref[...] = dm
    values = dm.astype(F32)
    centre = jnp.mean(values, axis=1, keepdims=True)
    off = values - centre
    spread = jnp.mean(off * off, axis=1, keepdims=True)
    normed = (off / jnp.sqrt(spread + EPSILON)).astype(BF16)
    before = jnp.concatenate([jnp.zeros((OWN, LANES), BF16), normed[:, : 3 * LANES]], axis=1)
    pairs = jnp.concatenate(
        [
            jnp.concatenate([before[:, k * LANES : (k + 1) * LANES], normed[:, k * LANES : (k + 1) * LANES]], axis=1)
            for k in range(TILES_OUT)
        ],
        axis=0,
    )
    best = [[] for _ in range(TILES_OUT)]
    for i in range(0, NBOX, 2):
        sums = dot(pairs, box[:, i * LANES : (i + 2) * LANES])
        for k in range(TILES_OUT):
            top = jnp.max(sums[k * OWN : (k + 1) * OWN].reshape(8, 8, 2 * LANES), axis=0)
            best[k] += [top[:, :LANES], top[:, LANES:]]
    rows = jnp.concatenate([jnp.max(jnp.stack(best[k], axis=0), axis=1) for k in range(TILES_OUT)] * 2, axis=0)
    found = jnp.max(rows.T, axis=0, keepdims=True)
    found = jnp.concatenate([found if k == 0 else pltpu.roll(found, LANES - k * NBOX, 1) for k in range(TILES_OUT)] * 2, axis=0)
    peaks[...] = found / root[...]

    for peer in band_peers:
        pltpu.make_async_remote_copy(
            src_ref=peaks, dst_ref=peaks_in.at[band],
            send_sem=peak_send, recv_sem=peak_recv,
            device_id=(me, peer), device_id_type=MESH,
        ).start()
    peaks_in[band] = peaks[...]
    for h in range(HALVES):
        arrived(block.at[h, pl.ds(0, BEAMS - 1)], beam_send.at[h])
        arrived(series.at[h, pl.ds(0, BANDS - 1)], band_send.at[h])
    arrived(peaks_in.at[pl.ds(0, BANDS - 1)], peak_recv)
    peak_ref[...] = jnp.max(peaks_in[...], axis=0)[:TILES_OUT, :NBOX]
    arrived(peaks_in.at[pl.ds(0, BANDS - 1)], peak_send)


def finish(dm_ref, peak_ref, dm_out, peak_out, sem):
    copies = [
        pltpu.make_async_copy(dm_ref, dm_out, sem.at[0]),
        pltpu.make_async_copy(peak_ref, peak_out, sem.at[1]),
    ]
    for copy in copies:
        copy.start()
    for copy in copies:
        copy.wait()


def local(intensity, chan_shift, sub_shift, widths):
    vmem = pl.BlockSpec(memory_space=pltpu.VMEM)
    operands = [pltpu.with_memory_space_constraint(a, pltpu.HBM) for a in (intensity, chan_shift, sub_shift, widths)]
    dm, peak = pl.pallas_call(
        kernel,
        out_shape=(
            jax.ShapeDtypeStruct((OWN, TILES_OUT * LANES), BF16),
            jax.ShapeDtypeStruct((TILES_OUT, NBOX), F32),
        ),
        in_specs=[pl.BlockSpec(memory_space=pltpu.HBM)] * 4,
        out_specs=(vmem, vmem),
        scratch_shapes=[
            pltpu.VMEM((HALVES, SAMPLES, BEAMS, LANES), BF16),
            pltpu.VMEM((GROUPS, 2 * LANES), jnp.int32),
            pltpu.SMEM((NBOX,), jnp.int32),
            pltpu.VMEM((HALVES, SAMPLES * BEAMS, LANES), F32),
            pltpu.VMEM((HALVES, BEAMS, SAMPLES, LANES), BF16),
            pltpu.VMEM((HALVES, BEAMS, SAMPLES, LANES), BF16),
            pltpu.VMEM((HALVES, GROUPS * 8, 2 * LANES), BF16),
            pltpu.VMEM((OWN, 256), jnp.int32),
            pltpu.VMEM((HALVES, SHIFTS * OWN, 256), BF16),
            pltpu.VMEM((HALVES, BANDS, TILES_MID, SUB_ROWS, LANES), BF16),
            pltpu.VMEM((HALVES, BANDS, TILES_MID, SUB_ROWS, LANES), BF16),
            pltpu.VMEM((256, NBOX * LANES), BF16),
            pltpu.VMEM((8, LANES), F32),
            pltpu.VMEM((OWN, TILES_OUT * LANES), F32),
            pltpu.VMEM((8, LANES), F32),
            pltpu.VMEM((BANDS, 8, LANES), F32),
            pltpu.SemaphoreType.DMA((5,)),
            pltpu.SemaphoreType.REGULAR,
            pltpu.SemaphoreType.DMA((HALVES,)),
            pltpu.SemaphoreType.DMA((HALVES, 2)),
            pltpu.SemaphoreType.DMA((HALVES,)),
            pltpu.SemaphoreType.DMA((HALVES, 2)),
            pltpu.SemaphoreType.DMA,
            pltpu.SemaphoreType.DMA,
        ],
        compiler_params=pltpu.CompilerParams(
            collective_id=0, has_side_effects=True, vmem_limit_bytes=48 << 20
        ),
        cost_estimate=pl.CostEstimate(flops=4_000_000_000, bytes_accessed=2_000_000, transcendentals=0),
    )(*operands)
    hbm = pl.BlockSpec(memory_space=pltpu.HBM)
    dm, peak = pl.pallas_call(
        finish,
        out_shape=(
            jax.ShapeDtypeStruct((OWN, TILES_OUT * LANES), BF16),
            jax.ShapeDtypeStruct((TILES_OUT, NBOX), F32),
        ),
        in_specs=[vmem, vmem],
        out_specs=(hbm, hbm),
        scratch_shapes=[pltpu.SemaphoreType.DMA((2,))],
        compiler_params=pltpu.CompilerParams(vmem_limit_bytes=16 << 20),
    )(dm, peak)
    return dm.reshape(OWN, 1, TILES_OUT * LANES), peak.T.reshape(1, NBOX, TILES_OUT)


def solution(mesh):
    return jax.shard_map(
        local,
        mesh=mesh,
        in_specs=(P("beam", None, "band"), P(None, "band"), P(), P()),
        out_specs=(P("band", "beam", None), P("beam", None, None)),
        check_vma=False,
    )
```

```python
import jax
import jax.numpy as jnp
from jax import lax
from jax.experimental import pallas as pl
from jax.experimental.pallas import tpu as pltpu
from jax.sharding import PartitionSpec as P

MESH = pl.DeviceIdType.MESH
F32 = jnp.float32
BF16 = jnp.bfloat16
LANES = 128
SAMPLES = 40
BEAMS = 32
RING = 16
AHEAD = 1
BANDS = 16
HALVES = 2
GROUPS = 32
SUB_ROWS = 16
TILES_IN = 10
TILES_MID = 9
TILES_OUT = 4
SHIFTS = 6
OWN = 64
NBOX = 16
EPSILON = 1e-05


def dot(a, b):
    return lax.dot_general(a, b, (((1,), (0,)), ((), ())), preferred_element_type=F32)


def dot_t(a, b):
    return lax.dot_general(a, b, (((1,), (1,)), ((), ())), preferred_element_type=F32)


def kernel(
    x_hbm, chan_hbm, shift_hbm, width_hbm, dm_ref, peak_ref,
    x_ref, chan_ref, width_ref, wide, block, got, chan_sel, shift_own, shift_sel, series, held, box, root, total, peaks, peaks_in,
    load_sem, ready, beam_send, beam_recv, band_send, band_recv, peak_send, peak_recv,
):
    me = lax.axis_index("beam")
    band = lax.axis_index("band")
    column = me // RING
    place = lax.rem(me, RING)

    band_x, band_y, core = band // 8, lax.rem(band // 2, 4), lax.rem(band, 2)
    band_peers = [
        lax.rem(band_x + x, 2) * 8 + lax.rem(band_y + y, 4) * 2 + lax.rem(core + c, 2)
        for x, y in ((1, 2), (1, 1), (1, 3), (0, 2), (1, 0), (0, 1), (0, 3), (0, 0))
        for c in (0, 1)
        if x or y or c
    ]

    barrier = pltpu.get_barrier_semaphore()

    def greet_beam(i, _):
        there = jnp.where(lax.rem(i, 2) == 1, (i + 1) // 2, lax.rem(RING - i // 2, RING))

        @pl.when(there != place)
        def _():
            pl.semaphore_signal(barrier, inc=1, device_id=(column * RING + there, band), device_id_type=MESH)

        @pl.when(column == 0)
        def _():
            pl.semaphore_signal(barrier, inc=1, device_id=(RING + there, band), device_id_type=MESH)

        return 0

    lax.fori_loop(0, RING, greet_beam, 0)

    def greet_band(i, _):
        pl.semaphore_signal(barrier, inc=1, device_id=(me, lax.rem(band + i, BANDS)), device_id_type=MESH)
        return 0

    lax.fori_loop(1, BANDS, greet_band, 0)

    loads = [
        pltpu.make_async_copy(x_hbm.at[:, :, pl.ds(h * LANES, LANES)], x_ref.at[h], load_sem.at[h]) for h in range(HALVES)
    ] + [
        pltpu.make_async_copy(chan_hbm, chan_ref, load_sem.at[2]),
        pltpu.make_async_copy(shift_hbm.at[pl.ds(band * OWN, OWN)], shift_own, load_sem.at[3]),
        pltpu.make_async_copy(width_hbm, width_ref, load_sem.at[4]),
    ]
    for load in loads:
        load.start()

    def gather(h):
        loads[h].wait()

        def widen(i, _):
            rows = pl.ds(pl.multiple_of(i * 8 * BEAMS, 8 * BEAMS), 8 * BEAMS)
            wide[h, rows, :] = x_ref[h, pl.ds(i * 8, 8)].astype(F32).reshape(8 * BEAMS, LANES)
            return 0

        lax.fori_loop(0, SAMPLES // 8, widen, 0)

        def pick(b, _):
            block[h, b] = wide.at[h][pl.ds(b, SAMPLES, stride=BEAMS), :].astype(BF16)
            return 0

        lax.fori_loop(0, BEAMS, pick, 0, unroll=4)
        got[h, me] = block[h, me]

    gather(0)
    pl.semaphore_wait(barrier, jnp.where(column == 0, RING, BEAMS) - 1 + BANDS - 1)

    @pl.when(column == 1)
    def _():
        pl.semaphore_signal(ready, inc=1, device_id=(place, band), device_id_type=MESH)


    def send_block(h, own, step):
        peer = lax.rem(column + 1 - own, 2) * RING + lax.rem(place + step + RING, RING)
        pltpu.make_async_remote_copy(
            src_ref=block.at[h, peer], dst_ref=got.at[h, me],
            send_sem=beam_send.at[h], recv_sem=beam_recv.at[h, own],
            device_id=(peer, band), device_id_type=MESH,
        ).start()

    def send_beams(h, own):
        def send(i, _):
            there = lax.rem(place + i, RING)

            @pl.when((h == 0) | (there >= AHEAD))
            def _():
                send_block(h, own, i)

            return 0

        lax.fori_loop(own, RING, send, 0)

    def send_ahead(there, _):
        send_block(1, 0, there - place)

        @pl.when(there != place)
        def _():
            send_block(1, 1, there - place)

        return 0

    send_beams(0, 1)
    gather(1)

    @pl.when(column == 0)
    def _():
        pl.semaphore_wait(ready, 1)

    send_beams(0, 0)
    lax.fori_loop(0, AHEAD, send_ahead, 0)
    send_beams(1, 0)

    loads[2].wait()
    loads[3].wait()
    loads[4].wait()

    row = lax.broadcasted_iota(jnp.int32, (GROUPS * 8, LANES), 0)
    lane = lax.broadcasted_iota(jnp.int32, (GROUPS * 8, LANES), 1)
    mine = lax.rem(row, 8) == lane // 16
    for h in range(HALVES):
        delays = chan_ref[:, h * LANES : (h + 1) * LANES]
        delays = jnp.broadcast_to(delays[:, None, :], (GROUPS, 8, LANES)).reshape(GROUPS * 8, LANES)
        for k in range(2):
            chan_sel[h, :, k * LANES : (k + 1) * LANES] = jnp.where(mine & (delays == k), 1.0, 0.0).astype(BF16)

    col = lax.broadcasted_iota(jnp.int32, (32, 256), 1)
    high = lax.rem(col // 8, 2) == 1
    for h in range(HALVES):
        first, second = shift_own[0:32, :], shift_own[32:64, :]
        if h == 0:
            second = pltpu.roll(second, 8, 1)
        else:
            first = pltpu.roll(first, 256 - 8, 1)
        for k in range(SHIFTS):
            shift_sel[h, k * OWN : k * OWN + 32, :] = jnp.where((first == k) & jnp.logical_not(high), 1.0, 0.0).astype(BF16)
            shift_sel[h, k * OWN + 32 : (k + 1) * OWN, :] = jnp.where((second == k) & high, 1.0, 0.0).astype(BF16)

    lag = (
        lax.broadcasted_iota(jnp.int32, (256, LANES), 1) + LANES
        - lax.broadcasted_iota(jnp.int32, (256, LANES), 0)
    )
    which = lax.broadcasted_iota(jnp.int32, (8, LANES), 1)
    scale = jnp.ones((8, LANES), F32)
    for i in range(NBOX):
        width = width_ref[i]
        box[:, i * LANES : (i + 1) * LANES] = jnp.where((lag >= 0) & (lag < width), 1.0, 0.0).astype(BF16)
        scale = jnp.where(which == i, width.astype(F32), scale)
    root[...] = jnp.sqrt(scale)

    total[...] = jnp.zeros_like(total)

    def arrived(buffer, sem):
        pltpu.make_async_copy(buffer, buffer, sem).wait()

    def tiles_of(h, side):
        return got[h, side * RING : (side + 1) * RING].astype(F32).reshape(RING * SAMPLES, LANES).astype(BF16)

    def channel_sum(h, now, later):
        return dot_t(chan_sel[h], jnp.concatenate([now, later], axis=1)).astype(BF16)

    def keep(h, first, summed):
        for i in range(summed.shape[1] // LANES):
            series[h, :, first + i] = summed[:, i * LANES : (i + 1) * LANES].reshape(BANDS, SUB_ROWS, LANES)

    def inner_tiles(h, side):
        data = got[h, pl.ds(side * RING, RING)].astype(F32).reshape(RING * SAMPLES, LANES).astype(BF16)
        keep(h, 5 * side, channel_sum(h, data[: 4 * LANES], data[LANES:]))

    def send_series(h, part, first, count):
        for peer in band_peers:
            pltpu.make_async_remote_copy(
                src_ref=series.at[h, peer, pl.ds(first, count)], dst_ref=held.at[h, band, pl.ds(first, count)],
                send_sem=band_send.at[h], recv_sem=band_recv.at[h, part],
                device_id=(me, peer), device_id_type=MESH,
            ).start()
        held[h, band, pl.ds(first, count)] = series[h, band, pl.ds(first, count)]

    def subseries(h, own, last):
        side = column if own else 1 - column
        arrived(got.at[h, pl.ds(0, RING - own)], beam_recv.at[h, own])
        inner_tiles(h, side)
        if last:
            keep(h, 4, channel_sum(h, tiles_of(h, 0)[4 * LANES :], tiles_of(h, 1)[:LANES]))
            send_series(h, 1, 4 * side, 5)
        else:
            send_series(h, 0, 5 * side, 4)

    def trials(h):
        arrived(held.at[h, pl.ds(0, BANDS - 1), pl.ds(0, 4)], band_recv.at[h, 0])
        arrived(held.at[h, pl.ds(0, BANDS - 1), pl.ds(0, 5)], band_recv.at[h, 1])
        for tile in range(0, TILES_MID, 2):
            tiles = [t for t in (tile, tile + 1) if t < TILES_MID]
            low = max(0, tiles[0] - TILES_OUT + 1)
            top = min(SHIFTS - 1, tiles[-1])
            data = jnp.concatenate([held[h, :, t].reshape(BANDS * SUB_ROWS, LANES) for t in tiles], axis=1)
            part = dot(shift_sel[h, low * OWN : (top + 1) * OWN, :], data)
            for n, t in enumerate(tiles):
                for k in range(low, top + 1):
                    o = t - k
                    if 0 <= o < TILES_OUT:
                        total[:, o * LANES : (o + 1) * LANES] += part[
                            (k - low) * OWN : (k - low + 1) * OWN, n * LANES : (n + 1) * LANES
                        ]

    subseries(0, 1, False)
    pl.when(place > 0)(lambda: send_beams(1, 1))
    subseries(0, 0, True)
    pl.when(place == 0)(lambda: send_beams(1, 1))
    trials(0)
    subseries(1, 0, False)
    subseries(1, 1, True)
    trials(1)

    dm = (total[...] * (1.0 / 64.0)).astype(BF16)
    dm_ref[...] = dm
    values = dm.astype(F32)
    centre = jnp.mean(values, axis=1, keepdims=True)
    off = values - centre
    spread = jnp.mean(off * off, axis=1, keepdims=True)
    normed = (off / jnp.sqrt(spread + EPSILON)).astype(BF16)
    before = jnp.concatenate([jnp.zeros((OWN, LANES), BF16), normed[:, : 3 * LANES]], axis=1)
    pairs = jnp.concatenate(
        [
            jnp.concatenate([before[:, k * LANES : (k + 1) * LANES], normed[:, k * LANES : (k + 1) * LANES]], axis=1)
            for k in range(TILES_OUT)
        ],
        axis=0,
    )
    best = [[] for _ in range(TILES_OUT)]
    for i in range(0, NBOX, 2):
        sums = dot(pairs, box[:, i * LANES : (i + 2) * LANES])
        for k in range(TILES_OUT):
            top = jnp.max(sums[k * OWN : (k + 1) * OWN].reshape(8, 8, 2 * LANES), axis=0)
            best[k] += [top[:, :LANES], top[:, LANES:]]
    rows = jnp.concatenate([jnp.max(jnp.stack(best[k], axis=0), axis=1) for k in range(TILES_OUT)] * 2, axis=0)
    found = jnp.max(rows.T, axis=0, keepdims=True)
    found = jnp.concatenate([found if k == 0 else pltpu.roll(found, LANES - k * NBOX, 1) for k in range(TILES_OUT)] * 2, axis=0)
    peaks[...] = found / root[...]

    for peer in band_peers:
        pltpu.make_async_remote_copy(
            src_ref=peaks, dst_ref=peaks_in.at[band],
            send_sem=peak_send, recv_sem=peak_recv,
            device_id=(me, peer), device_id_type=MESH,
        ).start()
    peaks_in[band] = peaks[...]
    for h in range(HALVES):
        arrived(block.at[h, pl.ds(0, BEAMS - 1)], beam_send.at[h])
        arrived(series.at[h, pl.ds(0, BANDS - 1)], band_send.at[h])
    arrived(peaks_in.at[pl.ds(0, BANDS - 1)], peak_recv)
    peak_ref[...] = jnp.max(peaks_in[...], axis=0)[:TILES_OUT, :NBOX]
    arrived(peaks_in.at[pl.ds(0, BANDS - 1)], peak_send)


def finish(dm_ref, peak_ref, dm_out, peak_out, sem):
    copies = [
        pltpu.make_async_copy(dm_ref, dm_out, sem.at[0]),
        pltpu.make_async_copy(peak_ref, peak_out, sem.at[1]),
    ]
    for copy in copies:
        copy.start()
    for copy in copies:
        copy.wait()


def local(intensity, chan_shift, sub_shift, widths):
    vmem = pl.BlockSpec(memory_space=pltpu.VMEM)
    operands = [pltpu.with_memory_space_constraint(a, pltpu.HBM) for a in (intensity, chan_shift, sub_shift, widths)]
    dm, peak = pl.pallas_call(
        kernel,
        out_shape=(
            jax.ShapeDtypeStruct((OWN, TILES_OUT * LANES), BF16),
            jax.ShapeDtypeStruct((TILES_OUT, NBOX), F32),
        ),
        in_specs=[pl.BlockSpec(memory_space=pltpu.HBM)] * 4,
        out_specs=(vmem, vmem),
        scratch_shapes=[
            pltpu.VMEM((HALVES, SAMPLES, BEAMS, LANES), BF16),
            pltpu.VMEM((GROUPS, 2 * LANES), jnp.int32),
            pltpu.SMEM((NBOX,), jnp.int32),
            pltpu.VMEM((HALVES, SAMPLES * BEAMS, LANES), F32),
            pltpu.VMEM((HALVES, BEAMS, SAMPLES, LANES), BF16),
            pltpu.VMEM((HALVES, BEAMS, SAMPLES, LANES), BF16),
            pltpu.VMEM((HALVES, GROUPS * 8, 2 * LANES), BF16),
            pltpu.VMEM((OWN, 256), jnp.int32),
            pltpu.VMEM((HALVES, SHIFTS * OWN, 256), BF16),
            pltpu.VMEM((HALVES, BANDS, TILES_MID, SUB_ROWS, LANES), BF16),
            pltpu.VMEM((HALVES, BANDS, TILES_MID, SUB_ROWS, LANES), BF16),
            pltpu.VMEM((256, NBOX * LANES), BF16),
            pltpu.VMEM((8, LANES), F32),
            pltpu.VMEM((OWN, TILES_OUT * LANES), F32),
            pltpu.VMEM((8, LANES), F32),
            pltpu.VMEM((BANDS, 8, LANES), F32),
            pltpu.SemaphoreType.DMA((5,)),
            pltpu.SemaphoreType.REGULAR,
            pltpu.SemaphoreType.DMA((HALVES,)),
            pltpu.SemaphoreType.DMA((HALVES, 2)),
            pltpu.SemaphoreType.DMA((HALVES,)),
            pltpu.SemaphoreType.DMA((HALVES, 2)),
            pltpu.SemaphoreType.DMA,
            pltpu.SemaphoreType.DMA,
        ],
        compiler_params=pltpu.CompilerParams(
            collective_id=0, has_side_effects=True, vmem_limit_bytes=48 << 20
        ),
        cost_estimate=pl.CostEstimate(flops=4_000_000_000, bytes_accessed=2_000_000, transcendentals=0),
    )(*operands)
    hbm = pl.BlockSpec(memory_space=pltpu.HBM)
    dm, peak = pl.pallas_call(
        finish,
        out_shape=(
            jax.ShapeDtypeStruct((OWN, TILES_OUT * LANES), BF16),
            jax.ShapeDtypeStruct((TILES_OUT, NBOX), F32),
        ),
        in_specs=[vmem, vmem],
        out_specs=(hbm, hbm),
        scratch_shapes=[pltpu.SemaphoreType.DMA((2,))],
        compiler_params=pltpu.CompilerParams(vmem_limit_bytes=16 << 20),
    )(dm, peak)
    return dm.reshape(OWN, 1, TILES_OUT * LANES), peak.T.reshape(1, NBOX, TILES_OUT)


def solution(mesh):
    return jax.shard_map(
        local,
        mesh=mesh,
        in_specs=(P("beam", None, "band"), P(None, "band"), P(), P()),
        out_specs=(P("band", "beam", None), P("beam", None, None)),
        check_vma=False,
    )
```
